32 devices in a mesh: seq: 8 (over z, core), head: 4 (over y, x).
Axes of the slice: x: 2, y: 2, z: 4, core: 2. Of those that a mesh axis runs over, the one named last changes fastest.
Arguments:
- queries: bfloat16 [8192, 4096], P('seq', 'head'), may hold values from -6 to 6
- key_rows: bfloat16 [8192, 4096], P('seq', 'head'), may hold values from -6 to 6
- value_rows: bfloat16 [8192, 4096], P('seq', 'head'), may hold values from -6 to 6
- out_weight: bfloat16 [4096, 4096], P('head'), may hold values from -0.375 to 0.375
- cotangent: bfloat16 [8192, 4096], P('seq', 'head'), may hold values from -1.5 to 1.5
- pattern: int32 [64, 6], P('seq'), may hold values 0 or 1
Outputs:
- output: bfloat16 [8192, 4096], P('seq', 'head')
- grad_query: bfloat16 [8192, 4096], P('seq', 'head')
- grad_keys: bfloat16 [8192, 4096], P('seq', 'head')
- grad_values: bfloat16 [8192, 4096], P('seq', 'head')
- grad_weight: float32 [4096, 4096], P('seq', 'head')
The draws below stay inside these ranges and needn't reach their ends.
All inputs are finite; a program needn't handle non-finite values. No bound on the sum of `pattern` on one device may be relied on, other than what follows from the above.
Results may differ from the reference program's by a relative error of at most 0.0076.
Values may be sent and summed in bfloat16 or wider, within the bound.
A program may use at most 256 MiB of HBM per device.

```python
import math
import jax
import jax.numpy as jnp
from jax import lax

D = 4096
HEADS = 32
DH = 128
BLK = 128
LEVELS = 6
TOKENS = 8192
NBLK = 64
HD = 4096


def query_key_pair(key):
    dims_all = (TOKENS, HEADS * DH)
    query_part = jax.random.truncated_normal(jax.random.fold_in(key, 21), -6.0, 6.0, dims_all, jnp.float32)
    key_part = jax.random.truncated_normal(jax.random.fold_in(key, 22), -6.0, 6.0, dims_all, jnp.float32)
    return (query_part, key_part)


def draw_queries(key, part):
    return query_key_pair(key)[0].astype(jnp.bfloat16)


def draw_key_rows(key, part):
    return query_key_pair(key)[1].astype(jnp.bfloat16)


def place_ends(values, own_key, least, largest):
    spot = [jax.random.randint(jax.random.fold_in(own_key, axis), (), 0, length) for axis, length in enumerate(values.shape)]
    longest = values.shape.index(max(values.shape))
    beside = spot[:longest] + [(spot[longest] + 1) % values.shape[longest]] + spot[longest + 1:]
    return values.at[tuple(spot)].set(least).at[tuple(beside)].set(largest)


def spiked(result, own_key, source, target, parts, factor):
    def block_of(position):
        return (jnp.arange(result.shape[position]) // (result.shape[position] // parts)).reshape((-1,) + (1,) * (result.ndim - 1 - position))

    first = jax.random.permutation(own_key, parts)[block_of(target)]
    second = (block_of(target) + parts // 2) % parts
    return jnp.where((block_of(source) == first) | (block_of(source) == second), factor * result, result)


def block_levels(stream_key, extent, cuts, low, high):
    factor_of, own = 1.0, jax.random.fold_in(stream_key, 6)
    for position, blocks in cuts:
        steps = jnp.exp(jax.random.uniform(jax.random.fold_in(own, position), (blocks,), jnp.float32, low / len(cuts), high / len(cuts)))
        factor_of = factor_of * jnp.repeat(steps, extent[position] // blocks).reshape([-1 if axis == position else 1 for axis in range(len(extent))])
    return factor_of


def bell_draw(rng, extent, scale, most, shards=(), kind=jnp.bfloat16):
    array = scale * jax.random.normal(rng, extent, jnp.float32)
    if shards:
        array = array * block_levels(rng, extent, shards, -0.22, 0.18)
    return jnp.clip(array, -most, most).astype(kind)


def heavy_noise(own_key, dims, spread, most, cuts, heavy, kind=jnp.bfloat16):
    values = spread * jax.random.normal(own_key, dims, jnp.float32)
    if cuts:
        values = values * block_levels(own_key, dims, cuts, -0.22, 0.18)
    return jnp.clip(spiked(values, jax.random.fold_in(own_key, 3), *heavy), -most, most).astype(kind)


def setup_inputs(seed: int = 0) -> dict:
    keys = jax.random.split(jax.random.key(seed), 7)
    queries = draw_queries(jax.random.fold_in(keys[6], 71), 0)
    key_rows = draw_key_rows(jax.random.fold_in(keys[6], 71), 0)
    value_rows = bell_draw(keys[2], (TOKENS, HD), 1.0, 6.0, ((0, 8), (1, 4)))
    out_weight = bell_draw(keys[3], (HD, D), (D // 16) ** -0.5, 0.375, ((0, 4),))
    cotangent = heavy_noise(keys[4], (TOKENS, D), 0.25, 1.5, ((0, 8), (1, 4)), (0, 1, 8, 2.0))
    pattern = place_ends((jax.random.randint(keys[5], (NBLK, LEVELS), 0, 4) < 3).astype(jnp.int32), jax.random.fold_in(keys[5], 1), 0, 1)
    return {"queries": queries, "key_rows": key_rows, "value_rows": value_rows, "out_weight": out_weight, "cotangent": cotangent, "pattern": pattern}


LOG_TWO = math.log(2.0)


def pool_rows(tensor, factor):
    return tensor.astype(jnp.float32).reshape(tensor.shape[0] // factor, factor, tensor.shape[1]).mean(axis=1)


def add_rows(target, start, extra):
    current = lax.dynamic_slice_in_dim(target, start, BLK, 0)
    return lax.dynamic_update_slice_in_dim(target, current + extra, start, 0)


def reference(queries, key_rows, value_rows, out_weight, cotangent, pattern):
    score_scale = DH ** -0.5
    grad_attn = jnp.dot(cotangent, out_weight.T, preferred_element_type=jnp.float32).astype(jnp.bfloat16)
    low_keys = [pool_rows(key_rows, 2 ** level_idx).astype(jnp.bfloat16) for level_idx in range(LEVELS)]
    low_vals = [pool_rows(value_rows, 2 ** level_idx).astype(jnp.bfloat16) for level_idx in range(LEVELS)]
    key_bias = jnp.concatenate([jnp.zeros((BLK,), jnp.float32)] + [jnp.full((BLK,), level_idx * LOG_TWO, jnp.float32) for level_idx in range(LEVELS)])
    keys_all = (1 + LEVELS) * BLK

    def visit(carried, block_idx):
        acc_keys, acc_vals = carried
        first_row = block_idx * BLK
        starts = [first_row] + [jnp.bitwise_xor(jnp.right_shift(block_idx, level_idx), 1) * BLK for level_idx in range(LEVELS)]
        key_set = jnp.concatenate([lax.dynamic_slice_in_dim(key_rows, first_row, BLK, 0)] + [lax.dynamic_slice_in_dim(low_keys[level_idx], starts[level_idx + 1], BLK, 0) for level_idx in range(LEVELS)], axis=0)
        val_set = jnp.concatenate([lax.dynamic_slice_in_dim(value_rows, first_row, BLK, 0)] + [lax.dynamic_slice_in_dim(low_vals[level_idx], starts[level_idx + 1], BLK, 0) for level_idx in range(LEVELS)], axis=0)
        level_flags = lax.dynamic_index_in_dim(pattern, block_idx, 0, keepdims=False) == 1
        kept_mask = jnp.concatenate([jnp.ones((BLK,), bool), jnp.repeat(level_flags, BLK)])
        query_heads = lax.dynamic_slice_in_dim(queries, first_row, BLK, 0).astype(jnp.float32).reshape(BLK, HEADS, DH)
        key_heads = key_set.astype(jnp.float32).reshape(keys_all, HEADS, DH)
        value_heads = val_set.astype(jnp.float32).reshape(keys_all, HEADS, DH)
        grad_heads = lax.dynamic_slice_in_dim(grad_attn, first_row, BLK, 0).astype(jnp.float32).reshape(BLK, HEADS, DH)
        scores = jnp.einsum('qhd,khd->hqk', query_heads, key_heads) * score_scale + key_bias
        scores = jnp.where(kept_mask, scores, -jnp.inf)
        row_max = jnp.max(scores, axis=-1, keepdims=True)
        weights_raw = jnp.exp(scores - row_max)
        attn_prob = weights_raw / jnp.sum(weights_raw, axis=-1, keepdims=True)
        prob_low = lax.optimization_barrier(attn_prob.astype(jnp.bfloat16)).astype(jnp.float32)
        attended_block = jnp.einsum('hqk,khd->qhd', prob_low, value_heads).astype(jnp.bfloat16).reshape(BLK, HD)
        grad_prob = jnp.einsum('qhd,khd->hqk', grad_heads, value_heads)
        row_delta = jnp.sum(attn_prob * grad_prob, axis=-1, keepdims=True)
        grad_score = lax.optimization_barrier((attn_prob * (grad_prob - row_delta)).astype(jnp.bfloat16)).astype(jnp.float32)
        grad_query_block = (jnp.einsum('hqk,khd->qhd', grad_score, key_heads) * score_scale).astype(jnp.bfloat16).reshape(BLK, HD)
        grad_keyset = (jnp.einsum('hqk,qhd->khd', grad_score, query_heads) * score_scale).reshape(keys_all, HD)
        grad_valset = jnp.einsum('hqk,qhd->khd', prob_low, grad_heads).reshape(keys_all, HD)
        acc_keys = list(acc_keys)
        acc_vals = list(acc_vals)
        acc_keys[0] = add_rows(acc_keys[0], first_row, grad_keyset[:BLK])
        acc_vals[0] = add_rows(acc_vals[0], first_row, grad_valset[:BLK])
        for level_idx in range(LEVELS):
            lower = (level_idx + 1) * BLK
            acc_keys[level_idx] = add_rows(acc_keys[level_idx], starts[level_idx + 1], grad_keyset[lower:lower + BLK])
            acc_vals[level_idx] = add_rows(acc_vals[level_idx], starts[level_idx + 1], grad_valset[lower:lower + BLK])
        return (acc_keys, acc_vals), (attended_block, grad_query_block)

    start_keys = [jnp.zeros((TOKENS // 2 ** level_idx, HD), jnp.float32) for level_idx in range(LEVELS)]
    start_vals = [jnp.zeros((TOKENS // 2 ** level_idx, HD), jnp.float32) for level_idx in range(LEVELS)]
    (acc_keys, acc_vals), (attended, grad_query) = lax.scan(visit, (start_keys, start_vals), jnp.arange(NBLK, dtype=jnp.int32))
    attended = attended.reshape(TOKENS, HD)
    grad_query = grad_query.reshape(TOKENS, HD)
    grad_keys = jnp.zeros((TOKENS, HD), jnp.float32)
    grad_values = jnp.zeros((TOKENS, HD), jnp.float32)
    for level_idx in range(LEVELS):
        factor = 2 ** level_idx
        grad_keys = grad_keys + jnp.repeat(acc_keys[level_idx], factor, axis=0) * (1.0 / factor)
        grad_values = grad_values + jnp.repeat(acc_vals[level_idx], factor, axis=0) * (1.0 / factor)
    output = jnp.dot(attended, out_weight, preferred_element_type=jnp.float32).astype(jnp.bfloat16)
    grad_weight = jnp.dot(cotangent.T, attended, preferred_element_type=jnp.float32)
    return output, grad_query, grad_keys.astype(jnp.bfloat16), grad_values.astype(jnp.bfloat16), grad_weight
```

```python
import functools
import math

import jax
import jax.numpy as jnp
from jax import lax
from jax.experimental import pallas as pl
from jax.experimental.pallas import tpu as pltpu
from jax.sharding import PartitionSpec as P

DH = 128
BLK = 128
PAIR = 2 * BLK
QUAD = 4 * BLK
SCALE = DH ** (-0.5)
LOG2E = 1.0 / math.log(2.0)
DROPPED = -1e30
VMEM = 44 * 1024 * 1024

NT = (((1,), (1,)), ((), ()))
TN = (((0,), (0,)), ((), ()))


def dot(left, right, dims=(((1,), (0,)), ((), ()))):
    return lax.dot_general(left, right, dims, preferred_element_type=jnp.float32)


def swapped(value, axis, mask):
    pairs = [(source, source ^ mask) for source in range(lax.axis_size(axis))]
    return lax.ppermute(value, axis, pairs)


def mean_matrix(rows, factor):
    group = lax.broadcasted_iota(jnp.int32, (rows, rows * factor), 0)
    token = lax.broadcasted_iota(jnp.int32, (rows, rows * factor), 1)
    return jnp.where(token // factor == group, 1.0 / factor, 0.0).astype(jnp.bfloat16)


def key_sets(rows, pool_two, pool_four, far):
    pairs = rows.shape[0] // PAIR
    quads = rows.shape[0] // QUAD
    twos = [
        dot(pool_two, rows[i * PAIR : (i + 1) * PAIR]).astype(jnp.bfloat16) for i in range(pairs)
    ]
    fours = [
        dot(pool_four, rows[i * QUAD : (i + 1) * QUAD]).astype(jnp.bfloat16) for i in range(quads)
    ]
    return [
        jnp.concatenate(
            [rows[i * PAIR : (i + 1) * PAIR], twos[i ^ 1], fours[(i >> 1) ^ 1], far], axis=0
        )
        for i in range(pairs)
    ]


def forward_kernel(q_ref, k_ref, v_ref, far_ref, two_ref, four_ref, bias_ref, prob_ref, out_ref):
    pool_two, pool_four = two_ref[...], four_ref[...]
    keys = key_sets(k_ref[...], pool_two, pool_four, far_ref[0])
    values = key_sets(v_ref[...], pool_two, pool_four, far_ref[1])
    for pair in range(len(keys)):
        span = slice(pair * PAIR, (pair + 1) * PAIR)
        scores = dot(keys[pair], q_ref[span, :], NT)
        parts = []
        for seg in range(scores.shape[0] // BLK):
            parts.append(
                scores[seg * BLK : (seg + 1) * BLK] * (SCALE * LOG2E)
                + bias_ref[pair, seg : seg + 1, :]
            )
        top = functools.reduce(jnp.maximum, [jnp.max(x, axis=0, keepdims=True) for x in parts])
        parts = [jnp.exp2(x - top) for x in parts]
        total = functools.reduce(jnp.add, [jnp.sum(x, axis=0, keepdims=True) for x in parts])
        scale = 1.0 / total
        prob = jnp.concatenate([(x * scale).astype(jnp.bfloat16) for x in parts], axis=0)
        prob_ref[0, pair] = prob
        out_ref[span, :] = dot(values[pair], prob, TN).T.astype(jnp.bfloat16)


def backward_kernel(
    q_ref, k_ref, v_ref, g_ref, far_ref, two_ref, four_ref, prob_ref, dq_ref, dk_ref, dv_ref, dfar_ref
):
    pool_two, pool_four = two_ref[...], four_ref[...]
    keys = key_sets(k_ref[...], pool_two, pool_four, far_ref[0])
    values = key_sets(v_ref[...], pool_two, pool_four, far_ref[1])
    grad_keys, grad_values = [], []
    for pair in range(len(keys)):
        span = slice(pair * PAIR, (pair + 1) * PAIR)
        grads = g_ref[span, :]
        grad_prob = dot(values[pair], grads, NT)
        prob_low = prob_ref[0, pair]
        prob = prob_low.astype(jnp.float32)
        delta = jnp.sum(prob * grad_prob, axis=0, keepdims=True)
        grad_score = (prob * (grad_prob - delta)).astype(jnp.bfloat16)
        dq_ref[span, :] = (dot(keys[pair], grad_score, TN) * SCALE).T.astype(jnp.bfloat16)
        grad_keys.append(dot(grad_score, q_ref[span, :]) * SCALE)
        grad_values.append(dot(prob_low, grads))
    for slot, (grad_sets, token_ref) in enumerate(((grad_keys, dk_ref), (grad_values, dv_ref))):
        dfar_ref[slot] = functools.reduce(
            jnp.add, [grad[PAIR + 2 * BLK :] for grad in grad_sets]
        ).astype(jnp.bfloat16)
        spread_four = []
        for quad in range(len(grad_sets) // 2):
            first = 2 * (quad ^ 1)
            node = sum(grad_sets[i][PAIR + BLK : PAIR + 2 * BLK] for i in (first, first + 1))
            spread_four.append(dot(pool_four, node.astype(jnp.bfloat16), TN))
        for pair in range(len(grad_sets)):
            node = grad_sets[pair ^ 1][PAIR : PAIR + BLK].astype(jnp.bfloat16)
            half = (pair & 1) * PAIR
            token_ref[pair * PAIR : (pair + 1) * PAIR, :] = (
                grad_sets[pair][:PAIR]
                + dot(pool_two, node, TN)
                + spread_four[pair >> 1][half : half + PAIR]
            )


def body(queries, key_rows, value_rows, out_weight, cotangent, pattern):
    rows, features = queries.shape
    width = out_weight.shape[1]
    blocks = rows // BLK
    pairs = blocks // 2
    seq_count = lax.axis_size("seq")
    head_axis = lax.axis_size("head")
    cross_levels = seq_count.bit_length() - 1
    heads = features // DH
    far_rows = cross_levels * BLK
    keys_all = PAIR + 2 * BLK + far_rows
    segments = keys_all // BLK
    where_seq = lax.axis_index("seq")
    where_head = lax.axis_index("head")
    messages = [
        (2**level + i, level, BLK >> level) for level in range(cross_levels) for i in range(2**level)
    ]

    grads_full = lax.all_gather(cotangent, "head", axis=1, tiled=True)

    pools = [mean_matrix(BLK >> level, blocks << level) for level in range(cross_levels)]
    far_own = []
    for pool in pools:
        far_own.append(
            jnp.stack([dot(pool, key_rows), dot(pool, value_rows)]).astype(jnp.bfloat16)
        )
    far = jnp.concatenate(
        [swapped(far_own[level], "seq", mask) for mask, level, _ in messages], axis=1
    )

    pool_two, pool_four = mean_matrix(BLK, 2), mean_matrix(BLK, 4)
    kept = jnp.where(
        pattern == 1, jnp.arange(pattern.shape[1], dtype=jnp.float32), DROPPED
    ).reshape(pairs, 2, pattern.shape[1])
    own = jnp.zeros((pairs, 1), jnp.float32)
    first = jnp.stack([own, kept[:, 1, :1]], axis=-1)
    second = jnp.stack([kept[:, 0, :1], own], axis=-1)
    bias = jnp.concatenate([first, second, kept[:, :, 1:].transpose(0, 2, 1)], axis=1)
    bias = jnp.repeat(bias, BLK, axis=2)

    column = pl.BlockSpec((rows, DH), lambda h: (0, h))
    far_spec = pl.BlockSpec((2, far_rows, DH), lambda h: (0, 0, h))
    two_spec = pl.BlockSpec((BLK, PAIR), lambda h: (0, 0))
    four_spec = pl.BlockSpec((BLK, QUAD), lambda h: (0, 0))
    prob_spec = pl.BlockSpec((1, pairs, keys_all, PAIR), lambda h: (h, 0, 0, 0))
    work = 2 * heads * pairs * keys_all * PAIR * DH

    prob, attended = pl.pallas_call(
        forward_kernel,
        grid=(heads,),
        out_shape=(
            jax.ShapeDtypeStruct((heads, pairs, keys_all, PAIR), jnp.bfloat16),
            jax.ShapeDtypeStruct((rows, features), jnp.bfloat16),
        ),
        in_specs=[
            column,
            column,
            column,
            far_spec,
            two_spec,
            four_spec,
            pl.BlockSpec((pairs, segments, PAIR), lambda h: (0, 0, 0)),
        ],
        out_specs=(prob_spec, column),
        compiler_params=pltpu.CompilerParams(vmem_limit_bytes=VMEM),
        cost_estimate=pl.CostEstimate(
            flops=12 * work, bytes_accessed=24 * rows * features, transcendentals=0
        ),
        name="forward_attention",
    )(queries, key_rows, value_rows, far, pool_two, pool_four, bias)

    output = None
    share = width // head_axis
    for mask in reversed(range(head_axis)):
        target = where_head ^ mask
        weight = lax.dynamic_slice_in_dim(out_weight, target * share, share, 1)
        partial = dot(attended, weight)
        if mask:
            partial = swapped(partial.astype(jnp.bfloat16), "head", mask).astype(jnp.float32)
        output = partial if output is None else output + partial
    output = output.astype(jnp.bfloat16)

    core = where_seq & 1
    chip = where_seq >> 1
    chips = seq_count // 2
    piece = width // seq_count
    by_core = grads_full.reshape(rows, chips, 2, piece)

    def weight_grad(which):
        chosen = lax.dynamic_index_in_dim(by_core, which, 2, keepdims=False)
        return dot(chosen.reshape(rows, chips * piece), attended, TN)

    theirs = swapped(weight_grad(1 - core).astype(jnp.bfloat16), "seq", 1)
    mine = weight_grad(core)
    grad_attn = dot(grads_full, out_weight, NT).astype(jnp.bfloat16)
    theirs, grad_attn = lax.optimization_barrier((theirs, grad_attn))
    mine = (mine + theirs.astype(jnp.float32)).astype(jnp.bfloat16)
    mine = mine.reshape(chips, piece, features)
    parts = [
        lax.dynamic_index_in_dim(mine, chip ^ mask, 0, keepdims=False) for mask in range(chips)
    ]
    parts, grad_attn = lax.optimization_barrier((parts, grad_attn))
    arrived = [swapped(parts[mask], "seq", 2 * mask) for mask in range(1, chips)]

    grad_query, dk, dv, dfar = pl.pallas_call(
        backward_kernel,
        grid=(heads,),
        out_shape=(
            jax.ShapeDtypeStruct((rows, features), jnp.bfloat16),
            jax.ShapeDtypeStruct((rows, features), jnp.float32),
            jax.ShapeDtypeStruct((rows, features), jnp.float32),
            jax.ShapeDtypeStruct((2, far_rows, features), jnp.bfloat16),
        ),
        in_specs=[column, column, column, column, far_spec, two_spec, four_spec, prob_spec],
        out_specs=(column, column, column, far_spec),
        compiler_params=pltpu.CompilerParams(vmem_limit_bytes=VMEM),
        cost_estimate=pl.CostEstimate(
            flops=16 * work, bytes_accessed=36 * rows * features, transcendentals=0
        ),
        name="backward_attention",
    )(queries, key_rows, value_rows, grad_attn, far, pool_two, pool_four, prob)

    arrived, dfar = lax.optimization_barrier((arrived, dfar))
    grad_weight = parts[0].astype(jnp.float32)
    for part in arrived:
        grad_weight = grad_weight + part.astype(jnp.float32)
    returned, at = [], 0
    for mask, level, count in messages:
        returned.append(swapped(dfar[:, at : at + count], "seq", mask))
        at += count
    returned = jnp.concatenate(returned, axis=1)
    spread = jnp.concatenate([pools[level] for _, level, _ in messages], axis=0)
    grad_keys = (dk + dot(spread, returned[0], TN)).astype(jnp.bfloat16)
    grad_values = (dv + dot(spread, returned[1], TN)).astype(jnp.bfloat16)
    return (output, grad_query, grad_keys, grad_values, grad_weight)


def solution(mesh):
    placed = (
        P("seq", "head"),
        P("seq", "head"),
        P("seq", "head"),
        P("head", None),
        P("seq", "head"),
        P("seq", None),
    )
    return jax.shard_map(
        body,
        mesh=mesh,
        in_specs=placed,
        out_specs=(
            P("seq", "head"),
            P("seq", "head"),
            P("seq", "head"),
            P("seq", "head"),
            P("seq", "head"),
        ),
        check_vma=False,
    )
```

```python
import functools
import math

import jax
import jax.numpy as jnp
from jax import lax
from jax.experimental import pallas as pl
from jax.experimental.pallas import tpu as pltpu
from jax.sharding import PartitionSpec as P

DH = 128
BLK = 128
PAIR = 2 * BLK
QUAD = 4 * BLK
SCALE = DH ** (-0.5)
LOG2E = 1.0 / math.log(2.0)
DROPPED = -1e30
VMEM = 44 * 1024 * 1024

NT = (((1,), (1,)), ((), ()))
TN = (((0,), (0,)), ((), ()))


def dot(left, right, dims=(((1,), (0,)), ((), ()))):
    return lax.dot_general(left, right, dims, preferred_element_type=jnp.float32)


def swapped(value, axis, mask):
    pairs = [(source, source ^ mask) for source in range(lax.axis_size(axis))]
    return lax.ppermute(value, axis, pairs)


def mean_matrix(rows, factor):
    group = lax.broadcasted_iota(jnp.int32, (rows, rows * factor), 0)
    token = lax.broadcasted_iota(jnp.int32, (rows, rows * factor), 1)
    return jnp.where(token // factor == group, 1.0 / factor, 0.0).astype(jnp.bfloat16)


def key_sets(rows, pool_two, pool_four, far):
    pairs = rows.shape[0] // PAIR
    quads = rows.shape[0] // QUAD
    twos = [
        dot(pool_two, rows[i * PAIR : (i + 1) * PAIR]).astype(jnp.bfloat16) for i in range(pairs)
    ]
    fours = [
        dot(pool_four, rows[i * QUAD : (i + 1) * QUAD]).astype(jnp.bfloat16) for i in range(quads)
    ]
    return [
        jnp.concatenate(
            [rows[i * PAIR : (i + 1) * PAIR], twos[i ^ 1], fours[(i >> 1) ^ 1], far], axis=0
        )
        for i in range(pairs)
    ]


def forward_kernel(q_ref, k_ref, v_ref, far_ref, two_ref, four_ref, bias_ref, prob_ref, out_ref):
    pool_two, pool_four = two_ref[...], four_ref[...]
    keys = key_sets(k_ref[...], pool_two, pool_four, far_ref[0])
    values = key_sets(v_ref[...], pool_two, pool_four, far_ref[1])
    for pair in range(len(keys)):
        span = slice(pair * PAIR, (pair + 1) * PAIR)
        scores = dot(keys[pair], q_ref[span, :], NT)
        parts = []
        for seg in range(scores.shape[0] // BLK):
            parts.append(
                scores[seg * BLK : (seg + 1) * BLK] * (SCALE * LOG2E)
                + bias_ref[pair, seg : seg + 1, :]
            )
        top = functools.reduce(jnp.maximum, [jnp.max(x, axis=0, keepdims=True) for x in parts])
        parts = [jnp.exp2(x - top) for x in parts]
        total = functools.reduce(jnp.add, [jnp.sum(x, axis=0, keepdims=True) for x in parts])
        scale = 1.0 / total
        prob = jnp.concatenate([(x * scale).astype(jnp.bfloat16) for x in parts], axis=0)
        prob_ref[0, pair] = prob
        out_ref[span, :] = dot(values[pair], prob, TN).T.astype(jnp.bfloat16)


def backward_kernel(
    q_ref, k_ref, v_ref, g_ref, far_ref, two_ref, four_ref, prob_ref, dq_ref, dk_ref, dv_ref, dfar_ref
):
    pool_two, pool_four = two_ref[...], four_ref[...]
    keys = key_sets(k_ref[...], pool_two, pool_four, far_ref[0])
    values = key_sets(v_ref[...], pool_two, pool_four, far_ref[1])
    grad_keys, grad_values = [], []
    for pair in range(len(keys)):
        span = slice(pair * PAIR, (pair + 1) * PAIR)
        grads = g_ref[span, :]
        grad_prob = dot(values[pair], grads, NT)
        prob_low = prob_ref[0, pair]
        prob = prob_low.astype(jnp.float32)
        delta = jnp.sum(prob * grad_prob, axis=0, keepdims=True)
        grad_score = (prob * (grad_prob - delta)).astype(jnp.bfloat16)
        dq_ref[span, :] = (dot(keys[pair], grad_score, TN) * SCALE).T.astype(jnp.bfloat16)
        grad_keys.append(dot(grad_score, q_ref[span, :]) * SCALE)
        grad_values.append(dot(prob_low, grads))
    for slot, (grad_sets, token_ref) in enumerate(((grad_keys, dk_ref), (grad_values, dv_ref))):
        dfar_ref[slot] = functools.reduce(
            jnp.add, [grad[PAIR + 2 * BLK :] for grad in grad_sets]
        ).astype(jnp.bfloat16)
        spread_four = []
        for quad in range(len(grad_sets) // 2):
            first = 2 * (quad ^ 1)
            node = sum(grad_sets[i][PAIR + BLK : PAIR + 2 * BLK] for i in (first, first + 1))
            spread_four.append(dot(pool_four, node.astype(jnp.bfloat16), TN))
        for pair in range(len(grad_sets)):
            node = grad_sets[pair ^ 1][PAIR : PAIR + BLK].astype(jnp.bfloat16)
            half = (pair & 1) * PAIR
            token_ref[pair * PAIR : (pair + 1) * PAIR, :] = (
                grad_sets[pair][:PAIR]
                + dot(pool_two, node, TN)
                + spread_four[pair >> 1][half : half + PAIR]
            )


def exchange_kernel(messages, source_ref, target_ref, send_sem, recv_sem):
    me = lax.axis_index("seq")
    peers = []
    for mask, _, _, _ in messages:
        peer, bit = me, 1
        while bit <= mask:
            if mask & bit:
                peer = peer + bit - 2 * bit * ((me // bit) % 2)
            bit *= 2
        peers.append(peer)
    barrier = pltpu.get_barrier_semaphore()
    for peer in peers:
        pl.semaphore_signal(
            barrier, inc=1, device_id={"seq": peer}, device_id_type=pl.DeviceIdType.MESH
        )
    pl.semaphore_wait(barrier, len(peers))
    copies = []
    for slot in reversed(range(len(messages))):
        _, source_at, target_at, count = messages[slot]
        copy = pltpu.make_async_remote_copy(
            src_ref=source_ref.at[:, pl.ds(source_at, count)],
            dst_ref=target_ref.at[:, pl.ds(target_at, count)],
            send_sem=send_sem.at[slot],
            recv_sem=recv_sem.at[slot],
            device_id={"seq": peers[slot]},
            device_id_type=pl.DeviceIdType.MESH,
        )
        copy.start()
        copies.append(copy)
    for copy in copies:
        copy.wait()


def exchange(source, messages, rows, ident):
    return pl.pallas_call(
        functools.partial(exchange_kernel, messages),
        out_shape=jax.ShapeDtypeStruct((2, rows, source.shape[2]), source.dtype),
        in_specs=[pl.BlockSpec(memory_space=pltpu.VMEM)],
        out_specs=pl.BlockSpec(memory_space=pltpu.VMEM),
        scratch_shapes=[
            pltpu.SemaphoreType.DMA((len(messages),)),
            pltpu.SemaphoreType.DMA((len(messages),)),
        ],
        compiler_params=pltpu.CompilerParams(
            collective_id=ident, has_side_effects=True, vmem_limit_bytes=16 * 1024 * 1024
        ),
        cost_estimate=pl.CostEstimate(flops=0, bytes_accessed=40 << 20, transcendentals=0),
        name="exchange",
    )(source)


def body(queries, key_rows, value_rows, out_weight, cotangent, pattern):
    rows, features = queries.shape
    width = out_weight.shape[1]
    blocks = rows // BLK
    pairs = blocks // 2
    seq_count = lax.axis_size("seq")
    head_axis = lax.axis_size("head")
    cross_levels = seq_count.bit_length() - 1
    heads = features // DH
    far_rows = cross_levels * BLK
    keys_all = PAIR + 2 * BLK + far_rows
    segments = keys_all // BLK
    where_seq = lax.axis_index("seq")
    where_head = lax.axis_index("head")
    head_masks = [mask for mask in range(1, head_axis)]
    chunks = [cotangent] + [swapped(cotangent, "head", mask) for mask in head_masks]

    outward, homeward, pools, at = [], [], [], 0
    for level in range(cross_levels):
        count = BLK >> level
        for i in range(2**level):
            outward.append((2**level + i, sum(BLK >> below for below in range(level)), at, count))
            homeward.append((2**level + i, at, at, count))
            at += count
        pools.append(mean_matrix(count, blocks << level))
    pool_far = jnp.concatenate(pools, axis=0)
    far_own = jnp.stack([dot(pool_far, key_rows), dot(pool_far, value_rows)]).astype(jnp.bfloat16)
    far = exchange(far_own, outward, far_rows, 1)

    pool_two, pool_four = mean_matrix(BLK, 2), mean_matrix(BLK, 4)
    kept = jnp.where(
        pattern == 1, jnp.arange(pattern.shape[1], dtype=jnp.float32), DROPPED
    ).reshape(pairs, 2, pattern.shape[1])
    own = jnp.zeros((pairs, 1), jnp.float32)
    first = jnp.stack([own, kept[:, 1, :1]], axis=-1)
    second = jnp.stack([kept[:, 0, :1], own], axis=-1)
    bias = jnp.concatenate([first, second, kept[:, :, 1:].transpose(0, 2, 1)], axis=1)
    bias = jnp.repeat(bias, BLK, axis=2)

    column = pl.BlockSpec((rows, DH), lambda h: (0, h))
    far_spec = pl.BlockSpec((2, far_rows, DH), lambda h: (0, 0, h))
    two_spec = pl.BlockSpec((BLK, PAIR), lambda h: (0, 0))
    four_spec = pl.BlockSpec((BLK, QUAD), lambda h: (0, 0))
    prob_spec = pl.BlockSpec((1, pairs, keys_all, PAIR), lambda h: (h, 0, 0, 0))
    work = 2 * heads * pairs * keys_all * PAIR * DH

    prob, attended = pl.pallas_call(
        forward_kernel,
        grid=(heads,),
        out_shape=(
            jax.ShapeDtypeStruct((heads, pairs, keys_all, PAIR), jnp.bfloat16),
            jax.ShapeDtypeStruct((rows, features), jnp.bfloat16),
        ),
        in_specs=[
            column,
            column,
            column,
            far_spec,
            two_spec,
            four_spec,
            pl.BlockSpec((pairs, segments, PAIR), lambda h: (0, 0, 0)),
        ],
        out_specs=(prob_spec, column),
        compiler_params=pltpu.CompilerParams(vmem_limit_bytes=VMEM),
        cost_estimate=pl.CostEstimate(
            flops=12 * work, bytes_accessed=24 * rows * features, transcendentals=0
        ),
        name="forward_attention",
    )(queries, key_rows, value_rows, far, pool_two, pool_four, bias)

    share = width // head_axis
    weights = [
        lax.dynamic_slice_in_dim(out_weight, (where_head ^ mask) * share, share, 1)
        for mask in range(head_axis)
    ]
    sums = [
        swapped(dot(attended, weights[mask]).astype(jnp.bfloat16), "head", mask)
        for mask in reversed(head_masks)
    ]
    own_sum = dot(attended, weights[0])

    core = where_seq & 1
    chip = where_seq >> 1
    chips = seq_count // 2
    piece = width // seq_count
    groups = chips // head_axis

    def weight_grad(which):
        chosen = [
            lax.dynamic_index_in_dim(
                chunk.reshape(rows, groups, 2, piece), which, 2, keepdims=False
            ).reshape(rows, groups * piece)
            for chunk in chunks
        ]
        return dot(jnp.concatenate(chosen, axis=1), attended, TN)

    theirs = swapped(weight_grad(1 - core).astype(jnp.bfloat16), "seq", 1)
    mine = (weight_grad(core) + theirs.astype(jnp.float32)).astype(jnp.bfloat16)
    mine = mine.reshape(chips, piece, features)
    parts = []
    for mask in range(chips):
        goal = chip ^ mask
        spot = ((goal // groups) ^ where_head) * groups + goal % groups
        parts.append(lax.dynamic_index_in_dim(mine, spot, 0, keepdims=False))
    parts, chunks = lax.optimization_barrier((parts, chunks))
    arrived = [swapped(parts[mask], "seq", 2 * mask) for mask in range(1, chips)]

    grad_attn = functools.reduce(
        jnp.add, [dot(chunk, weight, NT) for chunk, weight in zip(chunks, weights)]
    ).astype(jnp.bfloat16)

    grad_query, dk, dv, dfar = pl.pallas_call(
        backward_kernel,
        grid=(heads,),
        out_shape=(
            jax.ShapeDtypeStruct((rows, features), jnp.bfloat16),
            jax.ShapeDtypeStruct((rows, features), jnp.float32),
            jax.ShapeDtypeStruct((rows, features), jnp.float32),
            jax.ShapeDtypeStruct((2, far_rows, features), jnp.bfloat16),
        ),
        in_specs=[column, column, column, column, far_spec, two_spec, four_spec, prob_spec],
        out_specs=(column, column, column, far_spec),
        compiler_params=pltpu.CompilerParams(vmem_limit_bytes=VMEM),
        cost_estimate=pl.CostEstimate(
            flops=16 * work, bytes_accessed=36 * rows * features, transcendentals=0
        ),
        name="backward_attention",
    )(queries, key_rows, value_rows, grad_attn, far, pool_two, pool_four, prob)

    arrived, sums, dfar = lax.optimization_barrier((arrived, sums, dfar))
    grad_weight = parts[0].astype(jnp.float32)
    for part in arrived:
        grad_weight = grad_weight + part.astype(jnp.float32)
    output = own_sum
    for part in sums:
        output = output + part.astype(jnp.float32)
    output = output.astype(jnp.bfloat16)
    returned = exchange(dfar, homeward, far_rows, 2)
    spread = jnp.concatenate(
        [pool for level, pool in enumerate(pools) for _ in range(2**level)], axis=0
    )
    grad_keys = (dk + dot(spread, returned[0], TN)).astype(jnp.bfloat16)
    grad_values = (dv + dot(spread, returned[1], TN)).astype(jnp.bfloat16)
    return (output, grad_query, grad_keys, grad_values, grad_weight)


def solution(mesh):
    placed = (
        P("seq", "head"),
        P("seq", "head"),
        P("seq", "head"),
        P("head", None),
        P("seq", "head"),
        P("seq", None),
    )
    return jax.shard_map(
        body,
        mesh=mesh,
        in_specs=placed,
        out_specs=(
            P("seq", "head"),
            P("seq", "head"),
            P("seq", "head"),
            P("seq", "head"),
            P("seq", "head"),
        ),
        check_vma=False,
    )
```

```python
import functools
import math

import jax
import jax.numpy as jnp
from jax import lax
from jax.experimental import pallas as pl
from jax.experimental.pallas import tpu as pltpu
from jax.sharding import PartitionSpec as P

DH = 128
BLK = 128
PAIR = 2 * BLK
QUAD = 4 * BLK
SCALE = DH ** (-0.5)
LOG2E = 1.0 / math.log(2.0)
DROPPED = -1e30
VMEM = 44 * 1024 * 1024

NT = (((1,), (1,)), ((), ()))
TN = (((0,), (0,)), ((), ()))


def dot(left, right, dims=(((1,), (0,)), ((), ()))):
    return lax.dot_general(left, right, dims, preferred_element_type=jnp.float32)


def swapped(value, axis, mask):
    pairs = [(source, source ^ mask) for source in range(lax.axis_size(axis))]
    return lax.ppermute(value, axis, pairs)


def mean_matrix(rows, factor):
    group = lax.broadcasted_iota(jnp.int32, (rows, rows * factor), 0)
    token = lax.broadcasted_iota(jnp.int32, (rows, rows * factor), 1)
    return jnp.where(token // factor == group, 1.0 / factor, 0.0).astype(jnp.bfloat16)


def key_sets(rows, pool_two, pool_four, far):
    pairs = rows.shape[0] // PAIR
    quads = rows.shape[0] // QUAD
    twos = [
        dot(pool_two, rows[i * PAIR : (i + 1) * PAIR]).astype(jnp.bfloat16) for i in range(pairs)
    ]
    fours = [
        dot(pool_four, rows[i * QUAD : (i + 1) * QUAD]).astype(jnp.bfloat16) for i in range(quads)
    ]
    return [
        jnp.concatenate(
            [rows[i * PAIR : (i + 1) * PAIR], twos[i ^ 1], fours[(i >> 1) ^ 1], far], axis=0
        )
        for i in range(pairs)
    ]


def forward_kernel(q_ref, k_ref, v_ref, far_ref, two_ref, four_ref, bias_ref, prob_ref, out_ref):
    pool_two, pool_four = two_ref[...], four_ref[...]
    keys = key_sets(k_ref[...], pool_two, pool_four, far_ref[0])
    values = key_sets(v_ref[...], pool_two, pool_four, far_ref[1])
    for pair in range(len(keys)):
        span = slice(pair * PAIR, (pair + 1) * PAIR)
        scores = dot(keys[pair], q_ref[span, :], NT)
        parts = []
        for seg in range(scores.shape[0] // BLK):
            parts.append(
                scores[seg * BLK : (seg + 1) * BLK] * (SCALE * LOG2E)
                + bias_ref[pair, seg : seg + 1, :]
            )
        top = functools.reduce(jnp.maximum, [jnp.max(x, axis=0, keepdims=True) for x in parts])
        parts = [jnp.exp2(x - top) for x in parts]
        total = functools.reduce(jnp.add, [jnp.sum(x, axis=0, keepdims=True) for x in parts])
        scale = 1.0 / total
        prob = jnp.concatenate([(x * scale).astype(jnp.bfloat16) for x in parts], axis=0)
        prob_ref[0, pair] = prob
        out_ref[span, :] = dot(values[pair], prob, TN).T.astype(jnp.bfloat16)


def backward_kernel(
    q_ref, k_ref, v_ref, g_ref, far_ref, two_ref, four_ref, prob_ref, dq_ref, dk_ref, dv_ref, dfar_ref
):
    pool_two, pool_four = two_ref[...], four_ref[...]
    keys = key_sets(k_ref[...], pool_two, pool_four, far_ref[0])
    values = key_sets(v_ref[...], pool_two, pool_four, far_ref[1])
    grad_keys, grad_values = [], []
    for pair in range(len(keys)):
        span = slice(pair * PAIR, (pair + 1) * PAIR)
        grads = g_ref[span, :]
        grad_prob = dot(values[pair], grads, NT)
        prob_low = prob_ref[0, pair]
        prob = prob_low.astype(jnp.float32)
        delta = jnp.sum(prob * grad_prob, axis=0, keepdims=True)
        grad_score = (prob * (grad_prob - delta)).astype(jnp.bfloat16)
        dq_ref[span, :] = (dot(keys[pair], grad_score, TN) * SCALE).T.astype(jnp.bfloat16)
        grad_keys.append(dot(grad_score, q_ref[span, :]) * SCALE)
        grad_values.append(dot(prob_low, grads))
    for slot, (grad_sets, token_ref) in enumerate(((grad_keys, dk_ref), (grad_values, dv_ref))):
        dfar_ref[slot] = functools.reduce(
            jnp.add, [grad[PAIR + 2 * BLK :] for grad in grad_sets]
        ).astype(jnp.bfloat16)
        spread_four = []
        for quad in range(len(grad_sets) // 2):
            first = 2 * (quad ^ 1)
            node = sum(grad_sets[i][PAIR + BLK : PAIR + 2 * BLK] for i in (first, first + 1))
            spread_four.append(dot(pool_four, node.astype(jnp.bfloat16), TN))
        for pair in range(len(grad_sets)):
            node = grad_sets[pair ^ 1][PAIR : PAIR + BLK].astype(jnp.bfloat16)
            half = (pair & 1) * PAIR
            token_ref[pair * PAIR : (pair + 1) * PAIR, :] = (
                grad_sets[pair][:PAIR]
                + dot(pool_two, node, TN)
                + spread_four[pair >> 1][half : half + PAIR]
            )


def exchange_kernel(messages, source_ref, target_ref, send_sem, recv_sem):
    me = lax.axis_index("seq")
    peers = []
    for mask, _, _, _ in messages:
        peer, bit = me, 1
        while bit <= mask:
            if mask & bit:
                peer = peer + bit - 2 * bit * ((me // bit) % 2)
            bit *= 2
        peers.append(peer)
    barrier = pltpu.get_barrier_semaphore()
    for peer in peers:
        pl.semaphore_signal(
            barrier, inc=1, device_id={"seq": peer}, device_id_type=pl.DeviceIdType.MESH
        )
    pl.semaphore_wait(barrier, len(peers))
    copies = []
    for slot in reversed(range(len(messages))):
        _, source_at, target_at, count = messages[slot]
        copy = pltpu.make_async_remote_copy(
            src_ref=source_ref.at[:, pl.ds(source_at, count)],
            dst_ref=target_ref.at[:, pl.ds(target_at, count)],
            send_sem=send_sem.at[slot],
            recv_sem=recv_sem.at[slot],
            device_id={"seq": peers[slot]},
            device_id_type=pl.DeviceIdType.MESH,
        )
        copy.start()
        copies.append(copy)
    for copy in copies:
        copy.wait()


def exchange(source, messages, rows, ident):
    return pl.pallas_call(
        functools.partial(exchange_kernel, messages),
        out_shape=jax.ShapeDtypeStruct((2, rows, source.shape[2]), source.dtype),
        in_specs=[pl.BlockSpec(memory_space=pltpu.VMEM)],
        out_specs=pl.BlockSpec(memory_space=pltpu.VMEM),
        scratch_shapes=[
            pltpu.SemaphoreType.DMA((len(messages),)),
            pltpu.SemaphoreType.DMA((len(messages),)),
        ],
        compiler_params=pltpu.CompilerParams(
            collective_id=ident, has_side_effects=True, vmem_limit_bytes=16 * 1024 * 1024
        ),
        cost_estimate=pl.CostEstimate(flops=0, bytes_accessed=1 << 20, transcendentals=0),
        name="exchange",
    )(source)


def body(queries, key_rows, value_rows, out_weight, cotangent, pattern):
    rows, features = queries.shape
    width = out_weight.shape[1]
    blocks = rows // BLK
    pairs = blocks // 2
    seq_count = lax.axis_size("seq")
    head_axis = lax.axis_size("head")
    cross_levels = seq_count.bit_length() - 1
    heads = features // DH
    far_rows = cross_levels * BLK
    keys_all = PAIR + 2 * BLK + far_rows
    segments = keys_all // BLK
    where_seq = lax.axis_index("seq")
    where_head = lax.axis_index("head")
    head_masks = [mask for mask in range(1, head_axis)]
    chunks = [cotangent] + [swapped(cotangent, "head", mask) for mask in head_masks]

    outward, homeward, pools, at = [], [], [], 0
    for level in range(cross_levels):
        count = BLK >> level
        for i in range(2**level):
            outward.append((2**level + i, sum(BLK >> below for below in range(level)), at, count))
            homeward.append((2**level + i, at, at, count))
            at += count
        pools.append(mean_matrix(count, blocks << level))
    pool_far = jnp.concatenate(pools, axis=0)
    far_own = jnp.stack([dot(pool_far, key_rows), dot(pool_far, value_rows)]).astype(jnp.bfloat16)
    far = exchange(far_own, outward, far_rows, 1)

    pool_two, pool_four = mean_matrix(BLK, 2), mean_matrix(BLK, 4)
    kept = jnp.where(
        pattern == 1, jnp.arange(pattern.shape[1], dtype=jnp.float32), DROPPED
    ).reshape(pairs, 2, pattern.shape[1])
    own = jnp.zeros((pairs, 1), jnp.float32)
    first = jnp.stack([own, kept[:, 1, :1]], axis=-1)
    second = jnp.stack([kept[:, 0, :1], own], axis=-1)
    bias = jnp.concatenate([first, second, kept[:, :, 1:].transpose(0, 2, 1)], axis=1)
    bias = jnp.repeat(bias, BLK, axis=2)

    column = pl.BlockSpec((rows, DH), lambda h: (0, h))
    far_spec = pl.BlockSpec((2, far_rows, DH), lambda h: (0, 0, h))
    two_spec = pl.BlockSpec((BLK, PAIR), lambda h: (0, 0))
    four_spec = pl.BlockSpec((BLK, QUAD), lambda h: (0, 0))
    prob_spec = pl.BlockSpec((1, pairs, keys_all, PAIR), lambda h: (h, 0, 0, 0))
    work = 2 * heads * pairs * keys_all * PAIR * DH

    prob, attended = pl.pallas_call(
        forward_kernel,
        grid=(heads,),
        out_shape=(
            jax.ShapeDtypeStruct((heads, pairs, keys_all, PAIR), jnp.bfloat16),
            jax.ShapeDtypeStruct((rows, features), jnp.bfloat16),
        ),
        in_specs=[
            column,
            column,
            column,
            far_spec,
            two_spec,
            four_spec,
            pl.BlockSpec((pairs, segments, PAIR), lambda h: (0, 0, 0)),
        ],
        out_specs=(prob_spec, column),
        compiler_params=pltpu.CompilerParams(vmem_limit_bytes=VMEM),
        cost_estimate=pl.CostEstimate(
            flops=12 * work, bytes_accessed=24 * rows * features, transcendentals=0
        ),
        name="forward_attention",
    )(queries, key_rows, value_rows, far, pool_two, pool_four, bias)

    share = width // head_axis
    weights = [
        lax.dynamic_slice_in_dim(out_weight, (where_head ^ mask) * share, share, 1)
        for mask in range(head_axis)
    ]
    shares = [dot(attended, weight) for weight in weights]
    shares[1:] = [part.astype(jnp.bfloat16) for part in shares[1:]]
    shares, chunks = lax.optimization_barrier((shares, chunks))
    own_sum = shares[0]
    sums = [swapped(shares[mask], "head", mask) for mask in reversed(head_masks)]

    core = where_seq & 1
    chip = where_seq >> 1
    chips = seq_count // 2
    piece = width // seq_count
    groups = chips // head_axis
    full = [
        dot(chunk, attended, TN).astype(jnp.bfloat16).reshape(groups, 2, piece, features)
        for chunk in chunks
    ]

    def half(which):
        return jnp.concatenate(
            [lax.dynamic_index_in_dim(part, which, 1, keepdims=False) for part in full], axis=0
        )

    theirs = swapped(half(1 - core), "seq", 1)
    mine = (half(core).astype(jnp.float32) + theirs.astype(jnp.float32)).astype(jnp.bfloat16)
    parts = []
    for mask in range(chips):
        goal = chip ^ mask
        spot = ((goal // groups) ^ where_head) * groups + goal % groups
        parts.append(lax.dynamic_index_in_dim(mine, spot, 0, keepdims=False))
    parts, chunks = lax.optimization_barrier((parts, chunks))
    arrived = [swapped(parts[mask], "seq", 2 * mask) for mask in range(1, chips)]

    grad_attn = functools.reduce(
        jnp.add, [dot(chunk, weight, NT) for chunk, weight in zip(chunks, weights)]
    ).astype(jnp.bfloat16)

    grad_query, dk, dv, dfar = pl.pallas_call(
        backward_kernel,
        grid=(heads,),
        out_shape=(
            jax.ShapeDtypeStruct((rows, features), jnp.bfloat16),
            jax.ShapeDtypeStruct((rows, features), jnp.float32),
            jax.ShapeDtypeStruct((rows, features), jnp.float32),
            jax.ShapeDtypeStruct((2, far_rows, features), jnp.bfloat16),
        ),
        in_specs=[column, column, column, column, far_spec, two_spec, four_spec, prob_spec],
        out_specs=(column, column, column, far_spec),
        compiler_params=pltpu.CompilerParams(vmem_limit_bytes=VMEM),
        cost_estimate=pl.CostEstimate(
            flops=16 * work, bytes_accessed=36 * rows * features, transcendentals=0
        ),
        name="backward_attention",
    )(queries, key_rows, value_rows, grad_attn, far, pool_two, pool_four, prob)

    sums, dfar = lax.optimization_barrier((sums, dfar))
    returned = exchange(dfar, homeward, far_rows, 2)
    arrived, returned = lax.optimization_barrier((arrived, returned))
    grad_weight = parts[0].astype(jnp.float32)
    for part in arrived:
        grad_weight = grad_weight + part.astype(jnp.float32)
    output = own_sum
    for part in sums:
        output = output + part.astype(jnp.float32)
    output = output.astype(jnp.bfloat16)
    spread = jnp.concatenate(
        [pool for level, pool in enumerate(pools) for _ in range(2**level)], axis=0
    )
    grad_keys = (dk + dot(spread, returned[0], TN)).astype(jnp.bfloat16)
    grad_values = (dv + dot(spread, returned[1], TN)).astype(jnp.bfloat16)
    return (output, grad_query, grad_keys, grad_values, grad_weight)


def solution(mesh):
    placed = (
        P("seq", "head"),
        P("seq", "head"),
        P("seq", "head"),
        P("head", None),
        P("seq", "head"),
        P("seq", None),
    )
    return jax.shard_map(
        body,
        mesh=mesh,
        in_specs=placed,
        out_specs=(
            P("seq", "head"),
            P("seq", "head"),
            P("seq", "head"),
            P("seq", "head"),
            P("seq", "head"),
        ),
        check_vma=False,
    )
```

```python
import functools
import math

import jax
import jax.numpy as jnp
from jax import lax
from jax.experimental import pallas as pl
from jax.experimental.pallas import tpu as pltpu
from jax.sharding import PartitionSpec as P

DH = 128
BLK = 128
PAIR = 2 * BLK
QUAD = 4 * BLK
SCALE = DH ** (-0.5)
LOG2E = 1.0 / math.log(2.0)
DROPPED = -1e30
VMEM = 44 * 1024 * 1024

NT = (((1,), (1,)), ((), ()))
TN = (((0,), (0,)), ((), ()))


def dot(left, right, dims=(((1,), (0,)), ((), ()))):
    return lax.dot_general(left, right, dims, preferred_element_type=jnp.float32)


def swapped(value, axis, mask):
    pairs = [(source, source ^ mask) for source in range(lax.axis_size(axis))]
    return lax.ppermute(value, axis, pairs)


def mean_matrix(rows, factor):
    group = lax.broadcasted_iota(jnp.int32, (rows, rows * factor), 0)
    token = lax.broadcasted_iota(jnp.int32, (rows, rows * factor), 1)
    return jnp.where(token // factor == group, 1.0 / factor, 0.0).astype(jnp.bfloat16)


def key_sets(rows, pool_two, pool_four, far):
    pairs = rows.shape[0] // PAIR
    quads = rows.shape[0] // QUAD
    twos = [
        dot(pool_two, rows[i * PAIR : (i + 1) * PAIR]).astype(jnp.bfloat16) for i in range(pairs)
    ]
    fours = [
        dot(pool_four, rows[i * QUAD : (i + 1) * QUAD]).astype(jnp.bfloat16) for i in range(quads)
    ]
    return [
        jnp.concatenate(
            [rows[i * PAIR : (i + 1) * PAIR], twos[i ^ 1], fours[(i >> 1) ^ 1], far], axis=0
        )
        for i in range(pairs)
    ]


def forward_kernel(q_ref, k_ref, v_ref, far_ref, two_ref, four_ref, bias_ref, prob_ref, out_ref):
    pool_two, pool_four = two_ref[...], four_ref[...]
    keys = key_sets(k_ref[...], pool_two, pool_four, far_ref[0])
    values = key_sets(v_ref[...], pool_two, pool_four, far_ref[1])
    for pair in range(len(keys)):
        span = slice(pair * PAIR, (pair + 1) * PAIR)
        scores = dot(keys[pair], q_ref[span, :], NT)
        parts = []
        for seg in range(scores.shape[0] // BLK):
            parts.append(
                scores[seg * BLK : (seg + 1) * BLK] * (SCALE * LOG2E)
                + bias_ref[pair, seg : seg + 1, :]
            )
        top = functools.reduce(jnp.maximum, [jnp.max(x, axis=0, keepdims=True) for x in parts])
        parts = [jnp.exp2(x - top) for x in parts]
        total = functools.reduce(jnp.add, [jnp.sum(x, axis=0, keepdims=True) for x in parts])
        scale = 1.0 / total
        prob = jnp.concatenate([(x * scale).astype(jnp.bfloat16) for x in parts], axis=0)
        prob_ref[0, pair] = prob
        out_ref[span, :] = dot(values[pair], prob, TN).T.astype(jnp.bfloat16)


def backward_kernel(
    q_ref, k_ref, v_ref, g_ref, far_ref, two_ref, four_ref, prob_ref, dq_ref, dk_ref, dv_ref, dfar_ref
):
    pool_two, pool_four = two_ref[...], four_ref[...]
    keys = key_sets(k_ref[...], pool_two, pool_four, far_ref[0])
    values = key_sets(v_ref[...], pool_two, pool_four, far_ref[1])
    grad_keys, grad_values = [], []
    for pair in range(len(keys)):
        span = slice(pair * PAIR, (pair + 1) * PAIR)
        grads = g_ref[span, :]
        grad_prob = dot(values[pair], grads, NT)
        prob_low = prob_ref[0, pair]
        prob = prob_low.astype(jnp.float32)
        delta = jnp.sum(prob * grad_prob, axis=0, keepdims=True)
        grad_score = (prob * (grad_prob - delta)).astype(jnp.bfloat16)
        dq_ref[span, :] = (dot(keys[pair], grad_score, TN) * SCALE).T.astype(jnp.bfloat16)
        grad_keys.append(dot(grad_score, q_ref[span, :]) * SCALE)
        grad_values.append(dot(prob_low, grads))
    for slot, (grad_sets, token_ref) in enumerate(((grad_keys, dk_ref), (grad_values, dv_ref))):
        dfar_ref[slot] = functools.reduce(
            jnp.add, [grad[PAIR + 2 * BLK :] for grad in grad_sets]
        ).astype(jnp.bfloat16)
        spread_four = []
        for quad in range(len(grad_sets) // 2):
            first = 2 * (quad ^ 1)
            node = sum(grad_sets[i][PAIR + BLK : PAIR + 2 * BLK] for i in (first, first + 1))
            spread_four.append(dot(pool_four, node.astype(jnp.bfloat16), TN))
        for pair in range(len(grad_sets)):
            node = grad_sets[pair ^ 1][PAIR : PAIR + BLK].astype(jnp.bfloat16)
            half = (pair & 1) * PAIR
            token_ref[pair * PAIR : (pair + 1) * PAIR, :] = (
                grad_sets[pair][:PAIR]
                + dot(pool_two, node, TN)
                + spread_four[pair >> 1][half : half + PAIR]
            )


def exchange_kernel(messages, source_ref, target_ref, send_sem, recv_sem):
    me = lax.axis_index("seq")
    peers = []
    for mask, _, _, _ in messages:
        peer, bit = me, 1
        while bit <= mask:
            if mask & bit:
                peer = peer + bit - 2 * bit * ((me // bit) % 2)
            bit *= 2
        peers.append(peer)
    barrier = pltpu.get_barrier_semaphore()
    for peer in peers:
        pl.semaphore_signal(
            barrier, inc=1, device_id={"seq": peer}, device_id_type=pl.DeviceIdType.MESH
        )
    pl.semaphore_wait(barrier, len(peers))
    copies = []
    for slot in reversed(range(len(messages))):
        _, source_at, target_at, count = messages[slot]
        copy = pltpu.make_async_remote_copy(
            src_ref=source_ref.at[:, pl.ds(source_at, count)],
            dst_ref=target_ref.at[:, pl.ds(target_at, count)],
            send_sem=send_sem.at[slot],
            recv_sem=recv_sem.at[slot],
            device_id={"seq": peers[slot]},
            device_id_type=pl.DeviceIdType.MESH,
        )
        copy.start()
        copies.append(copy)
    for copy in copies:
        copy.wait()


def exchange(source, messages, rows, ident):
    return pl.pallas_call(
        functools.partial(exchange_kernel, messages),
        out_shape=jax.ShapeDtypeStruct((2, rows, source.shape[2]), source.dtype),
        in_specs=[pl.BlockSpec(memory_space=pltpu.VMEM)],
        out_specs=pl.BlockSpec(memory_space=pltpu.VMEM),
        scratch_shapes=[
            pltpu.SemaphoreType.DMA((len(messages),)),
            pltpu.SemaphoreType.DMA((len(messages),)),
        ],
        compiler_params=pltpu.CompilerParams(
            collective_id=ident, has_side_effects=True, vmem_limit_bytes=16 * 1024 * 1024
        ),
        cost_estimate=pl.CostEstimate(flops=0, bytes_accessed=1 << 20, transcendentals=0),
        name="exchange",
    )(source)


def body(queries, key_rows, value_rows, out_weight, cotangent, pattern):
    rows, features = queries.shape
    width = out_weight.shape[1]
    blocks = rows // BLK
    pairs = blocks // 2
    seq_count = lax.axis_size("seq")
    head_axis = lax.axis_size("head")
    cross_levels = seq_count.bit_length() - 1
    heads = features // DH
    far_rows = cross_levels * BLK
    keys_all = PAIR + 2 * BLK + far_rows
    segments = keys_all // BLK
    where_seq = lax.axis_index("seq")
    where_head = lax.axis_index("head")
    cut = rows // 2
    beside = swapped(cotangent, "head", 1)
    across = swapped(cotangent, "head", 2)

    outward, homeward, pools, at = [], [], [], 0
    for level in range(cross_levels):
        count = BLK >> level
        for i in range(2**level):
            outward.append((2**level + i, sum(BLK >> below for below in range(level)), at, count))
            homeward.append((2**level + i, at, at, count))
            at += count
        pools.append(mean_matrix(count, blocks << level))
    pool_far = jnp.concatenate(pools, axis=0)
    far_own = jnp.stack([dot(pool_far, key_rows), dot(pool_far, value_rows)]).astype(jnp.bfloat16)
    far = exchange(far_own, outward, far_rows, 1)
    far, beside, across = lax.optimization_barrier((far, beside, across))
    corner = jnp.concatenate(
        [swapped(across[:cut], "head", 1), swapped(beside[cut:], "head", 2)], axis=0
    )
    chunks = [cotangent, beside, across, corner]

    pool_two, pool_four = mean_matrix(BLK, 2), mean_matrix(BLK, 4)
    kept = jnp.where(
        pattern == 1, jnp.arange(pattern.shape[1], dtype=jnp.float32), DROPPED
    ).reshape(pairs, 2, pattern.shape[1])
    own = jnp.zeros((pairs, 1), jnp.float32)
    first = jnp.stack([own, kept[:, 1, :1]], axis=-1)
    second = jnp.stack([kept[:, 0, :1], own], axis=-1)
    bias = jnp.concatenate([first, second, kept[:, :, 1:].transpose(0, 2, 1)], axis=1)
    bias = jnp.repeat(bias, BLK, axis=2)

    column = pl.BlockSpec((rows, DH), lambda h: (0, h))
    far_spec = pl.BlockSpec((2, far_rows, DH), lambda h: (0, 0, h))
    two_spec = pl.BlockSpec((BLK, PAIR), lambda h: (0, 0))
    four_spec = pl.BlockSpec((BLK, QUAD), lambda h: (0, 0))
    prob_spec = pl.BlockSpec((1, pairs, keys_all, PAIR), lambda h: (h, 0, 0, 0))
    work = 2 * heads * pairs * keys_all * PAIR * DH

    prob, attended = pl.pallas_call(
        forward_kernel,
        grid=(heads,),
        out_shape=(
            jax.ShapeDtypeStruct((heads, pairs, keys_all, PAIR), jnp.bfloat16),
            jax.ShapeDtypeStruct((rows, features), jnp.bfloat16),
        ),
        in_specs=[
            column,
            column,
            column,
            far_spec,
            two_spec,
            four_spec,
            pl.BlockSpec((pairs, segments, PAIR), lambda h: (0, 0, 0)),
        ],
        out_specs=(prob_spec, column),
        compiler_params=pltpu.CompilerParams(vmem_limit_bytes=VMEM),
        cost_estimate=pl.CostEstimate(
            flops=work, bytes_accessed=2 * rows * features, transcendentals=0
        ),
        name="forward_attention",
    )(queries, key_rows, value_rows, far, pool_two, pool_four, bias)

    share = width // head_axis
    weights = [
        lax.dynamic_slice_in_dim(out_weight, (where_head ^ mask) * share, share, 1)
        for mask in range(head_axis)
    ]
    core = where_seq & 1
    chip = where_seq >> 1
    chips = seq_count // 2
    piece = width // seq_count
    groups = chips // head_axis
    chunks, attended = lax.optimization_barrier((chunks, attended))
    full = [
        dot(chunk, attended, TN).astype(jnp.bfloat16).reshape(groups, 2, piece, features)
        for chunk in chunks
    ]

    def half(which):
        return jnp.concatenate(
            [lax.dynamic_index_in_dim(part, which, 1, keepdims=False) for part in full], axis=0
        )

    theirs, attended = lax.optimization_barrier((half(1 - core), attended))
    theirs = swapped(theirs, "seq", 1)

    corner_sum = dot(attended, weights[3]).astype(jnp.bfloat16)
    passed_beside = swapped(corner_sum[:cut], "head", 1)
    passed_across = swapped(corner_sum[cut:], "head", 2)
    mine = (half(core).astype(jnp.float32) + theirs.astype(jnp.float32)).astype(jnp.bfloat16)
    mine, attended = lax.optimization_barrier((mine, attended))
    beside_sum = dot(attended, weights[1]).astype(jnp.bfloat16)
    across_sum = dot(attended, weights[2]).astype(jnp.bfloat16)
    own_sum = dot(attended, weights[0])

    def joined(whole, part):
        return (whole.astype(jnp.float32) + part.astype(jnp.float32)).astype(jnp.bfloat16)

    beside_sum = jnp.concatenate(
        [beside_sum[:cut], joined(beside_sum[cut:], passed_across)], axis=0
    )
    across_sum = jnp.concatenate(
        [joined(across_sum[:cut], passed_beside), across_sum[cut:]], axis=0
    )
    sums = [swapped(beside_sum, "head", 1), swapped(across_sum, "head", 2)]
    parts = []
    for mask in range(chips):
        goal = chip ^ mask
        spot = ((goal // groups) ^ where_head) * groups + goal % groups
        parts.append(lax.dynamic_index_in_dim(mine, spot, 0, keepdims=False))
    parts, chunks = lax.optimization_barrier((parts, chunks))
    arrived = [swapped(parts[mask], "seq", 2 * mask) for mask in range(1, chips)]

    grad_attn = functools.reduce(
        jnp.add, [dot(chunk, weight, NT) for chunk, weight in zip(chunks, weights)]
    ).astype(jnp.bfloat16)

    grad_query, dk, dv, dfar = pl.pallas_call(
        backward_kernel,
        grid=(heads,),
        out_shape=(
            jax.ShapeDtypeStruct((rows, features), jnp.bfloat16),
            jax.ShapeDtypeStruct((rows, features), jnp.float32),
            jax.ShapeDtypeStruct((rows, features), jnp.float32),
            jax.ShapeDtypeStruct((2, far_rows, features), jnp.bfloat16),
        ),
        in_specs=[column, column, column, column, far_spec, two_spec, four_spec, prob_spec],
        out_specs=(column, column, column, far_spec),
        compiler_params=pltpu.CompilerParams(vmem_limit_bytes=VMEM),
        cost_estimate=pl.CostEstimate(
            flops=work, bytes_accessed=2 * rows * features, transcendentals=0
        ),
        name="backward_attention",
    )(queries, key_rows, value_rows, grad_attn, far, pool_two, pool_four, prob)

    sums, dfar = lax.optimization_barrier((sums, dfar))
    returned = exchange(dfar, homeward, far_rows, 2)
    arrived, returned = lax.optimization_barrier((arrived, returned))
    grad_weight = parts[0].astype(jnp.float32)
    for part in arrived:
        grad_weight = grad_weight + part.astype(jnp.float32)
    output = own_sum
    for part in sums:
        output = output + part.astype(jnp.float32)
    output = output.astype(jnp.bfloat16)
    spread = jnp.concatenate(
        [pool for level, pool in enumerate(pools) for _ in range(2**level)], axis=0
    )
    grad_keys = (dk + dot(spread, returned[0], TN)).astype(jnp.bfloat16)
    grad_values = (dv + dot(spread, returned[1], TN)).astype(jnp.bfloat16)
    return (output, grad_query, grad_keys, grad_values, grad_weight)


def solution(mesh):
    placed = (
        P("seq", "head"),
        P("seq", "head"),
        P("seq", "head"),
        P("head", None),
        P("seq", "head"),
        P("seq", None),
    )
    return jax.shard_map(
        body,
        mesh=mesh,
        in_specs=placed,
        out_specs=(
            P("seq", "head"),
            P("seq", "head"),
            P("seq", "head"),
            P("seq", "head"),
            P("seq", "head"),
        ),
        check_vma=False,
    )
```
